128 devices in a mesh: rows: 32 (over y, z, core), cols: 4 (over x).
Axes of the slice: x: 4, y: 4, z: 4, core: 2. Of those that a mesh axis runs over, the one named last changes fastest.
Arguments:
- points: float32 [16, 1048576], P(None, ('rows', 'cols')), may hold values from -2 to 2
- coeffs: float32 [32, 1048576], P(None, ('rows', 'cols')), may hold values from -6 to 6
- velocity: float32 [32, 1048576], P(None, ('rows', 'cols')), may hold values from -4 to 4
- targets: float32 [32, 1048576], P(None, ('rows', 'cols')), may hold values from -6 to 6
- batch_index: int32 [2, 2048], replicated, may hold values from 0 to 1048575, as said below
- test_points: float32 [16, 4096], P(None, 'cols'), may hold values from -2 to 2
Outputs:
- coeffs_out: float32 [32, 1048576], P(None, ('rows', 'cols'))
- velocity_out: float32 [32, 1048576], P(None, ('rows', 'cols'))
- samples: float32 [32, 4096], P(None, 'cols')
The draws below stay inside these ranges and needn't reach their ends.
Inputs may be any that keep to these rules, and one draw needn't show every extreme that they name: `batch_index`: row numbers of training points, 2048 in each step; a row may repeat within a step, and rows of low-numbered devices are drawn far more often than others.
All inputs are finite; a program needn't handle non-finite values.
Results may differ from the reference program's by a relative error of at most 0.0042.
Values sent between devices are 32-bit elements; how exact they have to be, the bound alone decides.
No kernel may reach another device: no remote copies, remote signals or barrier semaphores. Data moves between devices by JAX's collectives and lax.ppermute only.
A program may use at most 128 MiB of HBM per device.

```python
import jax
import jax.numpy as jnp
from jax import lax

F = 16
S = 32
BATCH = 2048
STEPS = 2
TEST = 4096
ROWS_DEV = 8192
N = 1048576
N_ROWS = 32
N_COLS = 4


def draw_batch_index(key, part):
    owner_key = jax.random.fold_in(key, 11)
    row_key = jax.random.fold_in(key, 23)
    devices_all = N_ROWS * N_COLS
    spread = jax.random.randint(owner_key, (STEPS, BATCH), 0, devices_all)
    owner_dev = spread * spread // devices_all
    local_row = jax.random.randint(row_key, (STEPS, BATCH), 0, ROWS_DEV)
    picked = owner_dev * ROWS_DEV + local_row
    picked = picked.at[:, 0].set(N - 1).at[:, 1].set(0)
    return picked.astype(jnp.int32)


def shard_levels(stream_key, dims, cuts, smallest, largest):
    def one(position, blocks):
        draws = jax.random.uniform(jax.random.fold_in(jax.random.fold_in(stream_key, 6), position), (blocks,), jnp.float32, smallest / len(cuts), largest / len(cuts))
        return jnp.repeat(jnp.exp(draws), dims[position] // blocks).reshape((-1,) + (1,) * (len(dims) - position - 1))

    gain = one(*cuts[0])
    for cut in cuts[1:]:
        gain = gain * one(*cut)
    return gain


def noise(key, shape, scale, bound, shards=(), held_as=jnp.bfloat16):
    result = jax.random.normal(key, shape, jnp.float32) * scale
    if len(shards) > 0:
        result = shard_levels(key, shape, shards, -0.22, 0.18) * result
    return jnp.clip(result, min=-bound, max=bound).astype(held_as)


def setup_inputs(seed: int = 0) -> dict:
    key_of = jax.random.split(jax.random.key(seed), 7)
    points = jnp.clip(jax.random.uniform(key_of[0], (F, N), jnp.float32, -2.0, 2.0) * shard_levels(key_of[0], (F, N), ((1, 128),), -0.4, 0.0), -2.0, 2.0)
    coeffs = noise(key_of[1], (S, N), 1.0, 6.0, ((1, 128),), jnp.float32)
    velocity = noise(key_of[2], (S, N), 0.5, 4.0, ((1, 128),), jnp.float32)
    targets = noise(key_of[3], (S, N), 1.0, 6.0, ((1, 128),), jnp.float32)
    batch_index = draw_batch_index(jax.random.fold_in(key_of[6], 71), 0)
    test_points = jnp.clip(jax.random.uniform(key_of[5], (F, TEST), jnp.float32, -2.0, 2.0) * shard_levels(key_of[5], (F, TEST), ((1, 4),), -0.4, 0.0), -2.0, 2.0)
    return dict(points=points, coeffs=coeffs, velocity=velocity, targets=targets, batch_index=batch_index, test_points=test_points)


SCALE = 3.0 ** 0.5 / 1.25

def matern_tile(points_block, queries):
    cross_term = jnp.dot(points_block.T, queries, precision=lax.Precision.HIGHEST, preferred_element_type=jnp.float32)
    sq_points = lax.optimization_barrier(jnp.sum(points_block * points_block, axis=0))
    sq_queries = lax.optimization_barrier(jnp.sum(queries * queries, axis=0))
    dist_sq = jnp.maximum(sq_points[:, None] + sq_queries[None, :] - 2.0 * cross_term, 0.0)
    scaled = SCALE * jnp.sqrt(dist_sq)
    return ((1.0 + scaled) * jnp.exp(-scaled)).astype(jnp.bfloat16)

def kernel_sum(points, coeffs_now, queries):
    n_blocks = points.shape[1] // ROWS_DEV
    point_blocks = points.reshape(F, n_blocks, ROWS_DEV).transpose(1, 0, 2)
    coeff_blocks = coeffs_now.astype(jnp.bfloat16).reshape(S, n_blocks, ROWS_DEV).transpose(1, 0, 2)

    def add_block(total, pair):
        return (total + jnp.dot(pair[1], matern_tile(pair[0], queries), preferred_element_type=jnp.float32), None)
    start_total = jnp.zeros((S, queries.shape[1]), jnp.float32)
    total, unused = lax.scan(add_block, start_total, (point_blocks, coeff_blocks))
    return total

def reference(points, coeffs, velocity, targets, batch_index, test_points):
    coeffs_now = coeffs
    velocity_now = velocity
    for step_no in range(STEPS):
        picked = batch_index[step_no]
        batch_points = jnp.take(points, picked, axis=1)
        partial_sums = kernel_sum(points, coeffs_now, batch_points)
        gradient = partial_sums + 1.0 * jnp.take(coeffs_now, picked, axis=1) - jnp.take(targets, picked, axis=1)
        summed = jnp.zeros_like(coeffs_now).at[:, picked].add(gradient)
        velocity_now = 0.9 * velocity_now - 0.5 * summed
        coeffs_now = coeffs_now + velocity_now
    samples = kernel_sum(points, coeffs_now, test_points)
    return (coeffs_now, velocity_now, samples)
```

```python
import functools
import math

import jax
import jax.numpy as jnp
from jax import lax
from jax.experimental import pallas as pl
from jax.experimental.pallas import tpu as pltpu
from jax.sharding import PartitionSpec as P

BOTH = ("rows", "cols")
SCALE = 3.0**0.5 / 1.25
UNIT = SCALE / math.log(2.0)
SHIFT = 1.0 / math.log(2.0)
DROP = math.log2(math.log(2.0))
DEPTH = 128
WIDE = 256
F32 = jnp.float32
BF16 = jnp.bfloat16
VMEM_LIMIT = 48 << 20


def split(x, parts):
    pieces = []
    for _ in range(parts - 1):
        piece = x.astype(BF16)
        pieces.append(piece)
        x = x - piece.astype(F32)
    pieces.append(x.astype(BF16))
    return pieces


def tail_rows(norm_sq, norms_first):
    row = lax.broadcasted_iota(jnp.int32, (16, norm_sq.shape[1]), 0)
    base, ones = (0, 3) if norms_first else (3, 0)
    out = jnp.where((row >= ones) & (row < ones + 3), 1.0, 0.0)
    rest = norm_sq
    for piece_no in range(3):
        piece = rest.astype(BF16).astype(F32)
        out = jnp.where(row == base + piece_no, piece, out)
        rest = rest - piece
    return out.astype(BF16)


def point_side(points):
    x = points * UNIT
    a, b, c = split(x, 3)
    tail = tail_rows(jnp.sum(x * x, axis=0, keepdims=True), True)
    return jnp.concatenate([a, a, b, a, b, c, b, tail], axis=0)


def query_side(queries):
    x = queries * UNIT
    a, b, c = split(-2.0 * x, 3)
    tail = tail_rows(jnp.sum(x * x, axis=0, keepdims=True), False)
    return jnp.concatenate([a, b, a, c, b, a, c, tail], axis=0)


def transposed(x):
    return x.astype(F32).T.astype(BF16)


def matern(u_sq):
    u_sq = jnp.maximum(u_sq, 1e-12)
    u = u_sq * lax.rsqrt(u_sq)
    return (u + SHIFT) * jnp.exp2(DROP - u)


def last_dims(a, b):
    return lax.dot_general(a, b, (((1,), (1,)), ((), ())), preferred_element_type=F32)


def params():
    return pltpu.CompilerParams(vmem_limit_bytes=VMEM_LIMIT)


def cost(evaluations):
    return pl.CostEstimate(
        flops=evaluations * 1024, bytes_accessed=1 << 20, transcendentals=2 * evaluations
    )


def store_tiles(out_ref, value, lead):
    rows, columns = value.shape
    high = out_ref.shape[-2]
    for i in range(rows // high):
        for j in range(columns // 128):
            out_ref[lead(i, j)] = value[i * high : (i + 1) * high, j * 128 : (j + 1) * 128]


def prepare_kernel(points, coeffs, velocity, sides, halves):
    sides[...] = point_side(points[...])
    c = coeffs[...]
    halves[0] = c.astype(BF16)
    v = 0.9 * velocity[...]
    c = c + v
    halves[1] = c.astype(BF16)
    halves[2] = (c + 0.9 * v).astype(BF16)


def prepare(points, coeffs, velocity):
    feats, count = points.shape
    samples = coeffs.shape[0]
    blk = min(count, 1024)
    return pl.pallas_call(
        prepare_kernel,
        grid=(count // blk,),
        in_specs=[
            pl.BlockSpec((feats, blk), lambda i: (0, i)),
            pl.BlockSpec((samples, blk), lambda i: (0, i)),
            pl.BlockSpec((samples, blk), lambda i: (0, i)),
        ],
        out_specs=[
            pl.BlockSpec((DEPTH, blk), lambda i: (0, i)),
            pl.BlockSpec((3, samples, blk), lambda i: (0, 0, i)),
        ],
        out_shape=[
            jax.ShapeDtypeStruct((DEPTH, count), BF16),
            jax.ShapeDtypeStruct((3, samples, count), BF16),
        ],
        compiler_params=params(),
        name="prepare",
    )(points, coeffs, velocity)


def select_owned(stack, local, rows, parts):
    blocks = stack.shape[0] // rows
    q = local.shape[1]
    low = jnp.bitwise_and(local, WIDE - 1)
    high = jnp.right_shift(local, WIDE.bit_length() - 1)
    hot = (lax.broadcasted_iota(jnp.int32, (WIDE, q), 0) == low).astype(F32).astype(BF16)
    picked = jnp.dot(
        stack[...], jnp.concatenate([hot] * parts, axis=0), preferred_element_type=F32
    )
    total = jnp.zeros((rows, q), F32)
    for block in range(blocks):
        total = total + jnp.where(high == block, picked[block * rows : (block + 1) * rows], 0.0)
    return total


def fill_stack(stack, value_of, rows, parts):
    for block in range(stack.shape[0] // rows):
        pieces = split(value_of(slice(block * WIDE, (block + 1) * WIDE)), parts)
        for part, piece in enumerate(pieces):
            stack[block * rows : (block + 1) * rows, part * WIDE : (part + 1) * WIDE] = piece


def gather_points_kernel(start, index, points, out, stack):
    rows = points.shape[0]

    @pl.when(pl.program_id(0) == 0)
    def _():
        fill_stack(stack, lambda cols: points[:, cols], rows, 3)

    got = select_owned(stack, index[0] - start[0], rows, 3)
    store_tiles(out, got, lambda i, j: (i, j))


def gather_points(start, index, points):
    feats, count = points.shape
    steps, _, blk = index.shape
    return pl.pallas_call(
        gather_points_kernel,
        grid=(steps,),
        in_specs=[
            pl.BlockSpec(memory_space=pltpu.SMEM),
            pl.BlockSpec((1, 1, blk), lambda i: (i, 0, 0)),
            pl.BlockSpec((feats, count), lambda i: (0, 0)),
        ],
        out_specs=pl.BlockSpec((feats // 4, blk // 128, 4, 128), lambda i: (0, i, 0, 0)),
        out_shape=jax.ShapeDtypeStruct((feats // 4, steps * blk // 128, 4, 128), F32),
        scratch_shapes=[pltpu.VMEM((count // WIDE * feats, 3 * WIDE), BF16)],
        compiler_params=params(),
        name="gather_points",
    )(start, index, points)


def gather_terms_kernel(half_steps, start, index, coeffs, velocity, targets, out, stack):
    rows = coeffs.shape[0]

    @pl.when(pl.program_id(0) == 0)
    def _():
        fill_stack(stack, lambda cols: coeffs[:, cols] - targets[:, cols], rows, 2)

    @pl.when(pl.program_id(0) == half_steps)
    def _():
        fill_stack(
            stack,
            lambda cols: coeffs[:, cols] + 0.9 * velocity[:, cols] - targets[:, cols],
            rows,
            2,
        )

    got = select_owned(stack, index[0] - start[0], rows, 2)
    store_tiles(out, got, lambda i, j: (i, j))


def gather_terms(start, index, coeffs, velocity, targets):
    samples, count = coeffs.shape
    steps, _, blk = index.shape
    whole = pl.BlockSpec((samples, count), lambda i: (0, 0))
    return pl.pallas_call(
        functools.partial(gather_terms_kernel, steps // 2),
        grid=(steps,),
        in_specs=[
            pl.BlockSpec(memory_space=pltpu.SMEM),
            pl.BlockSpec((1, 1, blk), lambda i: (i, 0, 0)),
            whole,
            whole,
            whole,
        ],
        out_specs=pl.BlockSpec((samples // 8, blk // 128, 8, 128), lambda i: (0, i, 0, 0)),
        out_shape=jax.ShapeDtypeStruct((samples // 8, steps * blk // 128, 8, 128), F32),
        scratch_shapes=[pltpu.VMEM((count // WIDE * samples, 2 * WIDE), BF16)],
        compiler_params=params(),
        name="gather_terms",
    )(start, index, coeffs, velocity, targets)


def kernel_sums(side_t, sides, halves, chunk, unroll):
    count = sides.shape[1]
    q = side_t.shape[0]

    def step(i, acc):
        cols = pl.ds(pl.multiple_of(i * chunk, chunk), chunk)
        u_sq = jnp.dot(side_t[...], sides[:, cols], preferred_element_type=F32)
        return acc + last_dims(halves[:, cols], matern(u_sq).astype(BF16))

    return lax.fori_loop(
        0, count // chunk, step, jnp.zeros((halves.shape[0], q), F32), unroll=unroll
    )


def batch_kernel(queries, sides, halves, terms, out, side_t):
    side_t[...] = transposed(query_side(queries[...]))
    total = kernel_sums(side_t, sides, halves.at[0], 256, 16)
    for i in range(out.shape[0]):
        for j in range(out.shape[1]):
            out[i, j] = (
                total[i * 8 : (i + 1) * 8, j * 128 : (j + 1) * 128] + terms[i, j]
            )


def batch_sums(queries, sides, halves, terms):
    feats, total = queries.shape
    _, samples, count = halves.shape
    blk = 512
    steps = total // blk
    tile = pl.BlockSpec((samples // 8, blk // 128, 8, 128), lambda i: (0, i, 0, 0))
    return pl.pallas_call(
        batch_kernel,
        grid=(steps,),
        in_specs=[
            pl.BlockSpec((feats, blk), lambda i: (0, i)),
            pl.BlockSpec((DEPTH, count), lambda i: (0, 0)),
            pl.BlockSpec((1, samples, count), lambda i: (i // (steps // 2), 0, 0)),
            tile,
        ],
        out_specs=tile,
        out_shape=jax.ShapeDtypeStruct(terms.shape, F32),
        scratch_shapes=[pltpu.VMEM((blk, DEPTH), BF16)],
        compiler_params=params(),
        cost_estimate=cost(total * count),
        name="batch_sums",
    )(queries, sides, halves, terms)


def test_kernel(queries, sides, halves, *refs):
    out, side_t = refs[-2:]
    side_t[...] = transposed(query_side(queries[...]))
    total = kernel_sums(side_t, sides, halves.at[0], 256, 16)
    store_tiles(out, total, lambda i, j: (i, j, 0))


def test_sums(slab, n_slabs, queries, sides, halves, before):
    feats, total = queries.shape
    _, samples, count = halves.shape
    blk = 512
    per_slab = total // n_slabs
    steps = per_slab // blk
    in_specs = [
        pl.BlockSpec((feats, blk), lambda i: (0, slab * steps + i)),
        pl.BlockSpec((DEPTH, count), lambda i: (0, 0)),
        pl.BlockSpec((1, samples, count), lambda i: (2, 0, 0)),
    ]
    args = [queries, sides, halves]
    aliases = {}
    if before is not None:
        in_specs.append(pl.BlockSpec(memory_space=pl.ANY))
        args.append(before)
        aliases = {3: 0}
    return pl.pallas_call(
        test_kernel,
        grid=(steps,),
        in_specs=in_specs,
        out_specs=pl.BlockSpec(
            (samples // 8, blk // 128, 1, 8, 128), lambda i: (0, i, slab, 0, 0)
        ),
        out_shape=jax.ShapeDtypeStruct((samples // 8, per_slab // 128, n_slabs, 8, 128), F32),
        scratch_shapes=[pltpu.VMEM((blk, DEPTH), BF16)],
        input_output_aliases=aliases,
        compiler_params=params(),
        cost_estimate=cost(per_slab * count),
        name="test_sums",
    )(*args)


def second_kernel(queries, first, index0, index1, grad, sums, out, sides, weights, side_t, col):
    @pl.when(pl.program_id(0) == 0)
    def _():
        sides[...] = point_side(first[...])
        high, low = split(-0.5 * grad[...], 2)
        weights[...] = jnp.concatenate([high, low], axis=0)

    side_t[...] = transposed(query_side(queries[...]))
    blk = queries.shape[1]
    col[...] = jnp.broadcast_to(index1[0].astype(F32), (128, blk)).T
    chunk = 256

    def step(i, acc):
        cols = pl.ds(pl.multiple_of(i * chunk, chunk), chunk)
        u_sq = jnp.dot(side_t[...], sides[:, cols], preferred_element_type=F32)
        there = jnp.concatenate([col[...]] * (chunk // 128), axis=1)
        same = there == index0[0:1, cols].astype(F32)
        kern = matern(u_sq) + jnp.where(same, 1.0, 0.0)
        return acc + last_dims(weights[:, cols], kern.astype(BF16))

    total = lax.fori_loop(
        0, sides.shape[1] // chunk, step, jnp.zeros((weights.shape[0], blk), F32), unroll=True
    )
    half = weights.shape[0] // 2
    out[...] = sums[...] + total[:half] + total[half:]


def second_gradient(drawn, index, index_blocks, grad, sums):
    feats, total = drawn.shape
    samples, batch = grad.shape
    blk = 512
    steps = batch // blk
    return pl.pallas_call(
        second_kernel,
        grid=(steps,),
        in_specs=[
            pl.BlockSpec((feats, blk), lambda i: (0, steps + i)),
            pl.BlockSpec((feats, batch), lambda i: (0, 0)),
            pl.BlockSpec((2, batch), lambda i: (0, 0)),
            pl.BlockSpec((1, 1, blk), lambda i: (steps + i, 0, 0)),
            pl.BlockSpec((samples, batch), lambda i: (0, 0)),
            pl.BlockSpec((samples, blk), lambda i: (0, i)),
        ],
        out_specs=pl.BlockSpec((samples, blk), lambda i: (0, i)),
        out_shape=jax.ShapeDtypeStruct((samples, batch), F32),
        scratch_shapes=[
            pltpu.VMEM((DEPTH, batch), BF16),
            pltpu.VMEM((2 * samples, batch), BF16),
            pltpu.VMEM((blk, DEPTH), BF16),
            pltpu.VMEM((blk, 128), F32),
        ],
        compiler_params=params(),
        cost_estimate=cost(batch * batch),
        name="second_gradient",
    )(drawn, drawn, index, index_blocks, grad, sums)


def test_change_kernel(queries, drawn, grad0, grad1, out, sides, weights, side_t):
    batch = grad0.shape[1]

    @pl.when(pl.program_id(0) == 0)
    def _():
        sides[...] = point_side(drawn[...])
        for no, (grad, factor) in enumerate(((grad0, -0.95), (grad1, -0.5))):
            high, low = split(factor * grad[...], 2)
            weights[:, no * batch : (no + 1) * batch] = jnp.concatenate([high, low], axis=0)

    side_t[...] = transposed(query_side(queries[...]))
    total = kernel_sums(side_t, sides, weights, 256, True)
    half = weights.shape[0] // 2
    out[...] = total[:half] + total[half:]


def test_change(queries, drawn, grad0, grad1):
    feats, slab = queries.shape
    samples, batch = grad0.shape
    total = drawn.shape[1]
    blk = 512
    return pl.pallas_call(
        test_change_kernel,
        grid=(slab // blk,),
        in_specs=[
            pl.BlockSpec((feats, blk), lambda i: (0, i)),
            pl.BlockSpec((feats, total), lambda i: (0, 0)),
            pl.BlockSpec((samples, batch), lambda i: (0, 0)),
            pl.BlockSpec((samples, batch), lambda i: (0, 0)),
        ],
        out_specs=pl.BlockSpec((samples, blk), lambda i: (0, i)),
        out_shape=jax.ShapeDtypeStruct((samples, slab), F32),
        scratch_shapes=[
            pltpu.VMEM((DEPTH, total), BF16),
            pltpu.VMEM((2 * samples, total), BF16),
            pltpu.VMEM((blk, DEPTH), BF16),
        ],
        compiler_params=params(),
        cost_estimate=cost(total * slab),
        name="test_change",
    )(queries, drawn, grad0, grad1)


def update_kernel(
    start, index, coeffs, velocity, grad0, grad1, coeffs_out, velocity_out, hot, pieces, masked
):
    samples, batch = grad0.shape
    block_cols = coeffs.shape[1] // WIDE
    local = index[...] - start[0]
    high = jnp.right_shift(local, WIDE.bit_length() - 1)

    @pl.when(pl.program_id(0) == 0)
    def _():
        low = jnp.bitwise_and(local, WIDE - 1).astype(F32)
        lane = lax.broadcasted_iota(jnp.int32, (batch, 128), 1).astype(F32)
        for step, grad in enumerate((grad0, grad1)):
            column = jnp.broadcast_to(low[step : step + 1], (128, batch)).T
            for part in range(WIDE // 128):
                hot[step, :, part * 128 : (part + 1) * 128] = (
                    (column == lane + part * 128.0).astype(F32).astype(BF16)
                )
            first, second = split(grad[...], 2)
            pieces[step, :samples] = first
            pieces[step, samples:] = second

    first_block = pl.program_id(0) * block_cols
    sums = []
    for step in range(2):
        for block in range(block_cols):
            here = (high[step : step + 1] == first_block + block).astype(F32)
            here = jnp.broadcast_to(here, (16, batch)).astype(BF16)
            for part in range(2 * samples // 16):
                row = block * 2 * samples + part * 16
                masked[row : row + 16] = pieces[step, part * 16 : (part + 1) * 16] * here
        sums.append(jnp.dot(masked[...], hot[step], preferred_element_type=F32))
    for block in range(block_cols):
        cols = slice(block * WIDE, (block + 1) * WIDE)
        top = block * 2 * samples
        g0, g1 = (s[top : top + samples] + s[top + samples : top + 2 * samples] for s in sums)
        v1 = 0.9 * velocity[:, cols] - 0.5 * g0
        c1 = coeffs[:, cols] + v1
        v2 = 0.9 * v1 - 0.5 * g1
        velocity_out[:, cols] = v2
        coeffs_out[:, cols] = c1 + v2


def update(start, index, coeffs, velocity, grad0, grad1):
    samples, count = coeffs.shape
    batch = grad0.shape[1]
    blk = min(count, 2048)
    return pl.pallas_call(
        update_kernel,
        grid=(count // blk,),
        in_specs=[
            pl.BlockSpec(memory_space=pltpu.SMEM),
            pl.BlockSpec((2, batch), lambda i: (0, 0)),
            pl.BlockSpec((samples, blk), lambda i: (0, i)),
            pl.BlockSpec((samples, blk), lambda i: (0, i)),
            pl.BlockSpec((samples, batch), lambda i: (0, 0)),
            pl.BlockSpec((samples, batch), lambda i: (0, 0)),
        ],
        out_specs=[
            pl.BlockSpec((samples, blk), lambda i: (0, i)),
            pl.BlockSpec((samples, blk), lambda i: (0, i)),
        ],
        out_shape=[jax.ShapeDtypeStruct((samples, count), F32)] * 2,
        scratch_shapes=[
            pltpu.VMEM((2, batch, WIDE), BF16),
            pltpu.VMEM((2, 2 * samples, batch), BF16),
            pltpu.VMEM((blk // WIDE * 2 * samples, batch), BF16),
        ],
        compiler_params=params(),
        cost_estimate=pl.CostEstimate(
            flops=5 * 10**9, bytes_accessed=4 * samples * count * 4, transcendentals=0
        ),
        name="update",
    )(start, index, coeffs, velocity, grad0, grad1)


def scatter_sum(tiles, axes):
    return jnp.sum(lax.all_to_all(tiles, axes, 0, 0, tiled=True), axis=0)


def gather_all(tile, axes, size):
    copies = jnp.broadcast_to(tile[None], (size,) + tile.shape)
    return lax.all_to_all(copies, axes, 0, 0, tiled=True)


def from_tiles(tiles):
    i, j, high, wide = tiles.shape
    return tiles.transpose(0, 2, 1, 3).reshape(i * high, j * wide)


def after(value, *others):
    return lax.optimization_barrier((value,) + others)[0]


def per_device(n_rows, n_cols, points, coeffs, velocity, targets, batch_index, test_points):
    feats, count = points.shape
    samples = coeffs.shape[0]
    _, batch = batch_index.shape
    devices = n_rows * n_cols
    start = (lax.axis_index(BOTH) * count).astype(jnp.int32).reshape(1)
    blocks = batch_index.reshape(-1, 1, 512)

    mine = gather_points(start, blocks, points)
    test_mine = from_tiles_in(test_points)
    tests = gather_all(test_mine, "cols", n_cols)
    tests = tests.reshape(n_cols, 2, -1, 8, 128).transpose(1, 3, 0, 2, 4).reshape(feats, -1)
    sides, halves = prepare(points, coeffs, velocity)
    part = scatter_sum(mine.reshape(devices, 4, 128), BOTH)
    terms = gather_terms(start, blocks, coeffs, velocity, targets)
    test_part = test_sums(0, n_cols, tests, sides, halves, None)
    test_part = after(test_part, part, terms)
    drawn = gather_all(part, BOTH, devices)
    test_part = test_sums(1, n_cols, tests, sides, halves, test_part)
    drawn = after(drawn, test_part)
    drawn = from_tiles(drawn.reshape(mine.shape))

    sums = batch_sums(drawn, sides, halves, terms)
    test_part = after(test_part, sums)
    part = scatter_sum(sums.reshape(devices, 8, 128), BOTH)
    test_part = test_sums(2, n_cols, tests, sides, halves, test_part)
    test_part = after(test_part, part)
    sums = gather_all(part, BOTH, devices)
    test_part = test_sums(3, n_cols, tests, sides, halves, test_part)
    sums = from_tiles(sums.reshape(samples // 8, -1, 8, 128))
    grad0 = sums[:, :batch]

    test_part = scatter_sum(test_part.reshape(devices, 8, 128), BOTH)
    grad1 = second_gradient(drawn, batch_index, blocks, grad0, sums[:, batch:])
    change = test_change(test_points, drawn, grad0, grad1)
    coeffs_out, velocity_out = update(start, batch_index, coeffs, velocity, grad0, grad1)
    slab = gather_all(test_part, "rows", n_rows)
    slab = from_tiles(slab.reshape(samples // 8, -1, 8, 128)) + change
    return (coeffs_out, velocity_out, slab)


def from_tiles_in(x):
    rows, columns = x.shape
    return (
        x.reshape(rows // 8, 8, columns // 128, 128).transpose(0, 2, 1, 3).reshape(-1, 8, 128)
    )


def solution(mesh):
    n_rows, n_cols = mesh.shape["rows"], mesh.shape["cols"]
    return jax.shard_map(
        functools.partial(per_device, n_rows, n_cols),
        mesh=mesh,
        in_specs=(
            P(None, BOTH),
            P(None, BOTH),
            P(None, BOTH),
            P(None, BOTH),
            P(),
            P(None, "cols"),
        ),
        out_specs=(P(None, BOTH), P(None, BOTH), P(None, "cols")),
        check_vma=False,
    )
```

```python
import functools
import math

import jax
import jax.numpy as jnp
from jax import lax
from jax.experimental import pallas as pl
from jax.experimental.pallas import tpu as pltpu
from jax.sharding import PartitionSpec as P

BOTH = ("rows", "cols")
SCALE = 3.0**0.5 / 1.25
UNIT = SCALE / math.log(2.0)
SHIFT = 1.0 / math.log(2.0)
DROP = math.log2(math.log(2.0))
DEPTH = 192
WIDE = 256
PARTS = 1
F32 = jnp.float32
BF16 = jnp.bfloat16
VMEM_LIMIT = 40 << 20


def split(x, parts):
    pieces = []
    for _ in range(parts - 1):
        piece = x.astype(BF16)
        pieces.append(piece)
        x = x - piece.astype(F32)
    pieces.append(x.astype(BF16))
    return pieces


def side(points, scale):
    x = points * UNIT
    return split(scale * x, 3), split(x * x, 3)


def point_side(points):
    (a, b, c), squares = side(points, 1.0)
    one = jnp.ones(a.shape, BF16)
    return jnp.concatenate([a, a, b, a, b, c] + squares + [one] * 3, axis=0)


def query_side(queries):
    (a, b, c), squares = side(queries, -2.0)
    one = jnp.ones(a.shape, BF16)
    return jnp.concatenate([a, b, a, c, b, a] + [one] * 3 + squares, axis=0)


def transposed(x):
    return x.astype(F32).T.astype(BF16)


def matern(u_sq):
    u_sq = jnp.maximum(u_sq, 1e-12)
    u = u_sq * lax.rsqrt(u_sq)
    return (u + SHIFT) * jnp.exp2(DROP - u)


def last_dims(a, b):
    return lax.dot_general(a, b, (((1,), (1,)), ((), ())), preferred_element_type=F32)


def hbm(x):
    return pltpu.with_memory_space_constraint(x, pltpu.HBM)


def params():
    return pltpu.CompilerParams(vmem_limit_bytes=VMEM_LIMIT)


def cost(evaluations):
    return pl.CostEstimate(
        flops=evaluations * 1024, bytes_accessed=1 << 20, transcendentals=2 * evaluations
    )


def lanes(tiles):
    return jnp.concatenate([tiles[i] for i in range(tiles.shape[0])], axis=1)


def store_columns(out, value):
    for i in range(out.shape[0]):
        out[i] = value[:, i * 128 : (i + 1) * 128]


def prepare_kernel(points, coeffs, velocity, sides, halves):
    sides[...] = point_side(points[...])
    c = coeffs[...]
    halves[0] = c.astype(BF16)
    v = 0.9 * velocity[...]
    c = c + v
    halves[1] = c.astype(BF16)
    halves[2] = (c + 0.9 * v).astype(BF16)


def prepare(points, coeffs, velocity):
    feats, count = points.shape
    samples = coeffs.shape[0]
    blk = min(count, 1024)
    return pl.pallas_call(
        prepare_kernel,
        grid=(count // blk,),
        in_specs=[
            pl.BlockSpec((feats, blk), lambda i: (0, i)),
            pl.BlockSpec((samples, blk), lambda i: (0, i)),
            pl.BlockSpec((samples, blk), lambda i: (0, i)),
        ],
        out_specs=[
            pl.BlockSpec((DEPTH, blk), lambda i: (0, i)),
            pl.BlockSpec((3, samples, blk), lambda i: (0, 0, i)),
        ],
        out_shape=[
            pltpu.HBM((DEPTH, count), BF16),
            pltpu.HBM((3, samples, count), BF16),
        ],
        compiler_params=params(),
        name="prepare",
    )(hbm(points), hbm(coeffs), hbm(velocity))


def select_owned(stack, local, rows, parts):
    blocks = stack.shape[0] // rows
    q = local.shape[1]
    low = jnp.bitwise_and(local, WIDE - 1)
    high = jnp.right_shift(local, WIDE.bit_length() - 1)
    hot = (lax.broadcasted_iota(jnp.int32, (WIDE, q), 0) == low).astype(F32).astype(BF16)
    picked = jnp.dot(
        stack[...], jnp.concatenate([hot] * parts, axis=0), preferred_element_type=F32
    )
    total = jnp.zeros((rows, q), F32)
    for block in range(blocks):
        total = total + jnp.where(high == block, picked[block * rows : (block + 1) * rows], 0.0)
    return total


def fill_stack(stack, value_of, rows, parts):
    for block in range(stack.shape[0] // rows):
        pieces = split(value_of(slice(block * WIDE, (block + 1) * WIDE)), parts)
        for part, piece in enumerate(pieces):
            stack[block * rows : (block + 1) * rows, part * WIDE : (part + 1) * WIDE] = piece


def index_part(index, out):
    q = out.shape[0] * 128
    per_row = index.shape[1] // q
    step = pl.program_id(0)
    first = pl.multiple_of(lax.rem(step, per_row) * q, q)
    both = index[:, pl.ds(first, q)]
    return jnp.where(step < per_row, both[0:1], both[1:2])


def gather_points_kernel(start, index, points, out, stack):
    rows = points.shape[0]

    @pl.when(pl.program_id(0) == 0)
    def _():
        fill_stack(stack, lambda cols: points[:, cols], rows, 3)

    store_columns(out, select_owned(stack, index_part(index, out) - start[0], rows, 3))


def gather_points(start, index, points):
    feats, count = points.shape
    blk = 1024
    steps = index.size // blk
    return pl.pallas_call(
        gather_points_kernel,
        grid=(steps,),
        in_specs=[
            pl.BlockSpec(memory_space=pltpu.SMEM),
            pl.BlockSpec(index.shape, lambda i: (0, 0)),
            pl.BlockSpec((feats, count), lambda i: (0, 0)),
        ],
        out_specs=pl.BlockSpec((blk // 128, feats, 128), lambda i: (i, 0, 0)),
        out_shape=jax.ShapeDtypeStruct((steps * blk // 128, feats, 128), F32),
        scratch_shapes=[pltpu.VMEM((count // WIDE * feats, 3 * WIDE), BF16)],
        compiler_params=params(),
        name="gather_points",
    )(start, index, hbm(points))


def gather_terms_kernel(half_steps, start, index, coeffs, velocity, targets, out, stack):
    rows = coeffs.shape[0]

    @pl.when(pl.program_id(0) == 0)
    def _():
        fill_stack(stack, lambda cols: coeffs[:, cols] - targets[:, cols], rows, 2)

    @pl.when(pl.program_id(0) == half_steps)
    def _():
        fill_stack(
            stack,
            lambda cols: coeffs[:, cols] + 0.9 * velocity[:, cols] - targets[:, cols],
            rows,
            2,
        )

    store_columns(out, select_owned(stack, index_part(index, out) - start[0], rows, 2))


def gather_terms(start, index, coeffs, velocity, targets):
    samples, count = coeffs.shape
    blk = 1024
    steps = index.size // blk
    whole = pl.BlockSpec((samples, count), lambda i: (0, 0))
    return pl.pallas_call(
        functools.partial(gather_terms_kernel, steps // 2),
        grid=(steps,),
        in_specs=[
            pl.BlockSpec(memory_space=pltpu.SMEM),
            pl.BlockSpec(index.shape, lambda i: (0, 0)),
            whole,
            whole,
            whole,
        ],
        out_specs=pl.BlockSpec((blk // 128, samples, 128), lambda i: (i, 0, 0)),
        out_shape=jax.ShapeDtypeStruct((steps * blk // 128, samples, 128), F32),
        scratch_shapes=[pltpu.VMEM((count // WIDE * samples, 2 * WIDE), BF16)],
        compiler_params=params(),
        name="gather_terms",
    )(start, index, hbm(coeffs), hbm(velocity), hbm(targets))


def kernel_sums(side_t, sides, halves, chunk, unroll):
    count = sides.shape[1]
    q = side_t.shape[0]

    def step(i, acc):
        cols = pl.ds(pl.multiple_of(i * chunk, chunk), chunk)
        u_sq = jnp.dot(side_t[...], sides[:, cols], preferred_element_type=F32)
        return acc + last_dims(halves[:, cols], matern(u_sq).astype(BF16))

    return lax.fori_loop(
        0, count // chunk, step, jnp.zeros((halves.shape[0], q), F32), unroll=unroll
    )


def dense_step(queries_of, sides, halves, side_t, acc):
    part = pl.program_id(1)

    @pl.when(part == 0)
    def _():
        side_t[...] = transposed(query_side(queries_of()))
        acc[...] = jnp.zeros(acc.shape, F32)

    acc[...] += kernel_sums(side_t, sides, halves.at[0], 256, 16)
    return part == pl.num_programs(1) - 1


def dense_scratch(samples, blk):
    return [pltpu.VMEM((blk, DEPTH), BF16), pltpu.VMEM((samples, blk), F32)]


def batch_kernel(queries, sides, halves, terms, out, side_t, acc):
    @pl.when(dense_step(lambda: lanes(queries), sides, halves, side_t, acc))
    def _():
        for i in range(out.shape[0]):
            out[i] = acc[:, i * 128 : (i + 1) * 128] + terms[i]


def batch_sums(drawn, sides, halves, terms):
    tiles, feats, _ = drawn.shape
    _, samples, count = halves.shape
    wide = 16
    steps = tiles // wide
    part = count // PARTS
    tile = pl.BlockSpec((wide, samples, 128), lambda i, k: (i, 0, 0))
    return pl.pallas_call(
        batch_kernel,
        grid=(steps, PARTS),
        in_specs=[
            pl.BlockSpec((wide, feats, 128), lambda i, k: (i, 0, 0)),
            pl.BlockSpec((DEPTH, part), lambda i, k: (0, k)),
            pl.BlockSpec((1, samples, part), lambda i, k: (i // (steps // 2), 0, k)),
            tile,
        ],
        out_specs=tile,
        out_shape=jax.ShapeDtypeStruct(terms.shape, F32),
        scratch_shapes=dense_scratch(samples, wide * 128),
        compiler_params=params(),
        cost_estimate=cost(tiles * 128 * count),
        name="batch_sums",
    )(drawn, hbm(sides), hbm(halves), terms)


def test_kernel(own, slab, queries, sides, halves, *refs):
    out, side_t, acc = refs[-3:]

    def queries_of():
        return queries[...] if own else lanes(queries)

    @pl.when(dense_step(queries_of, sides, halves, side_t, acc))
    def _():
        for i in range(out.shape[0]):
            for j in range(out.shape[1]):
                out[i, j, 0] = acc[i * 8 : (i + 1) * 8, j * 128 : (j + 1) * 128]


def test_sums(slab, offset, n_slabs, per_slab, many, queries, sides, halves, before):
    _, samples, count = halves.shape
    part = count // PARTS
    own = before is None
    slab_tiles = per_slab // 128

    def which(i, slab_ref):
        return lax.rem(slab_ref[0] + offset + i, n_slabs)

    if own:
        first = pl.BlockSpec((queries.shape[0], per_slab), lambda i, k, s: (0, 0))
    else:
        first = pl.BlockSpec(
            (slab_tiles, queries.shape[1], 128), lambda i, k, s: (which(i, s), 0, 0)
        )
    in_specs = [
        first,
        pl.BlockSpec((DEPTH, part), lambda i, k, s: (0, k)),
        pl.BlockSpec((1, samples, part), lambda i, k, s: (2, 0, k)),
    ]
    args = [queries, hbm(sides), hbm(halves)]
    aliases = {}
    if not own:
        in_specs.append(pl.BlockSpec(memory_space=pl.ANY))
        args.append(before)
        aliases = {4: 0}
    return pl.pallas_call(
        functools.partial(test_kernel, own),
        grid_spec=pltpu.PrefetchScalarGridSpec(
            num_scalar_prefetch=1,
            grid=(many, PARTS),
            in_specs=in_specs,
            out_specs=pl.BlockSpec(
                (samples // 8, slab_tiles, 1, 8, 128),
                lambda i, k, s: (0, 0, which(i, s), 0, 0),
            ),
            scratch_shapes=dense_scratch(samples, per_slab),
        ),
        out_shape=jax.ShapeDtypeStruct((samples // 8, slab_tiles, n_slabs, 8, 128), F32),
        input_output_aliases=aliases,
        compiler_params=params(),
        cost_estimate=cost(many * per_slab * count),
        name="test_sums",
    )(slab, *args)


def tile_rows(tiles, i):
    return jnp.concatenate([tiles[i, j] for j in range(tiles.shape[1])], axis=0)


def second_kernel(drawn, index, received, grad0, grad1, sides, weights, side_t, col):
    batch = index.shape[1]
    tiles = batch // 128
    for tile in range(tiles):
        cols = slice(tile * 128, (tile + 1) * 128)
        sides[:, cols] = point_side(drawn[tile])
        side_t[cols, :] = transposed(query_side(drawn[tiles + tile]))
        g = tile_rows(received, tile)
        grad0[:, cols] = g
        weights[:, cols] = jnp.concatenate(split(-0.5 * g, 2), axis=0)
    col[...] = jnp.broadcast_to(index[1:2, :].astype(F32), (128, batch)).T
    chunk = 256
    total = jnp.zeros((weights.shape[0], batch), F32)
    for first in range(0, batch, chunk):
        cols = slice(first, first + chunk)
        u_sq = jnp.dot(side_t[...], sides[:, cols], preferred_element_type=F32)
        there = jnp.concatenate([col[...]] * (chunk // 128), axis=1)
        same = jnp.where(there == index[0:1, cols].astype(F32), 1.0, 0.0)
        kern = (matern(u_sq) + same).astype(BF16)
        total = total + last_dims(weights[:, cols], kern)
    half = weights.shape[0] // 2
    total = total[:half] + total[half:]
    for tile in range(tiles):
        cols = slice(tile * 128, (tile + 1) * 128)
        grad1[:, cols] = tile_rows(received, tiles + tile) + total[:, cols]


def second_gradient(drawn, index, received):
    batch = index.shape[1]
    samples = received.shape[1] * received.shape[2]
    return pl.pallas_call(
        second_kernel,
        out_shape=[jax.ShapeDtypeStruct((samples, batch), F32)] * 2,
        scratch_shapes=[
            pltpu.VMEM((DEPTH, batch), BF16),
            pltpu.VMEM((2 * samples, batch), BF16),
            pltpu.VMEM((batch, DEPTH), BF16),
            pltpu.VMEM((batch, 128), F32),
        ],
        compiler_params=params(),
        cost_estimate=cost(batch * batch),
        name="second_gradient",
    )(drawn, index, received)


def test_change_kernel(queries, drawn, grad0, grad1, dense, out, sides, weights, side_t):
    batch = grad0.shape[1]
    for tile in range(drawn.shape[0]):
        sides[:, tile * 128 : (tile + 1) * 128] = point_side(drawn[tile])
    for no, (grad, factor) in enumerate(((grad0, -0.95), (grad1, -0.5))):
        high, low = split(factor * grad[...], 2)
        weights[:, no * batch : (no + 1) * batch] = jnp.concatenate([high, low], axis=0)
    side_t[...] = transposed(query_side(queries[...]))
    change = kernel_sums(side_t, sides, weights, 256, 8)
    half = weights.shape[0] // 2
    change = change[:half] + change[half:]
    for i in range(dense.shape[0]):
        for j in range(dense.shape[1]):
            rows, cols = slice(i * 8, (i + 1) * 8), slice(j * 128, (j + 1) * 128)
            out[rows, cols] = change[rows, cols] + dense[i, j]


def test_change(queries, drawn, grad0, grad1, dense):
    slab = queries.shape[1]
    samples = grad0.shape[0]
    total = drawn.shape[0] * 128
    return pl.pallas_call(
        test_change_kernel,
        out_shape=jax.ShapeDtypeStruct((samples, slab), F32),
        scratch_shapes=[
            pltpu.VMEM((DEPTH, total), BF16),
            pltpu.VMEM((2 * samples, total), BF16),
            pltpu.VMEM((slab, DEPTH), BF16),
        ],
        compiler_params=params(),
        cost_estimate=cost(total * slab),
        name="test_change",
    )(queries, drawn, grad0, grad1, dense)


def update_kernel(
    start, index, coeffs, velocity, grad0, grad1, coeffs_out, velocity_out, hot, pieces, masked
):
    samples, batch = grad0.shape
    block_cols = coeffs.shape[1] // WIDE
    local = index[...] - start[0]
    high = jnp.right_shift(local, WIDE.bit_length() - 1)

    @pl.when(pl.program_id(0) == 0)
    def _():
        low = jnp.bitwise_and(local, WIDE - 1).astype(F32)
        lane = lax.broadcasted_iota(jnp.int32, (batch, 128), 1).astype(F32)
        for step, grad in enumerate((grad0, grad1)):
            column = jnp.broadcast_to(low[step : step + 1], (128, batch)).T
            for part in range(WIDE // 128):
                hot[step, :, part * 128 : (part + 1) * 128] = (
                    (column == lane + part * 128.0).astype(F32).astype(BF16)
                )
            first, second = split(grad[...], 2)
            pieces[step, :samples] = first
            pieces[step, samples:] = second

    first_block = pl.program_id(0) * block_cols
    sums = []
    for step in range(2):
        for block in range(block_cols):
            here = (high[step : step + 1] == first_block + block).astype(F32)
            here = jnp.broadcast_to(here, (16, batch)).astype(BF16)
            for part in range(2 * samples // 16):
                row = block * 2 * samples + part * 16
                masked[row : row + 16] = pieces[step, part * 16 : (part + 1) * 16] * here
        sums.append(jnp.dot(masked[...], hot[step], preferred_element_type=F32))
    for block in range(block_cols):
        cols = slice(block * WIDE, (block + 1) * WIDE)
        top = block * 2 * samples
        g0, g1 = (s[top : top + samples] + s[top + samples : top + 2 * samples] for s in sums)
        v1 = 0.9 * velocity[:, cols] - 0.5 * g0
        c1 = coeffs[:, cols] + v1
        v2 = 0.9 * v1 - 0.5 * g1
        velocity_out[:, cols] = v2
        coeffs_out[:, cols] = c1 + v2


def update(start, index, coeffs, velocity, grad0, grad1):
    samples, count = coeffs.shape
    batch = grad0.shape[1]
    blk = min(count, 2048)
    return pl.pallas_call(
        update_kernel,
        grid=(count // blk,),
        in_specs=[
            pl.BlockSpec(memory_space=pltpu.SMEM),
            pl.BlockSpec((2, batch), lambda i: (0, 0)),
            pl.BlockSpec((samples, blk), lambda i: (0, i)),
            pl.BlockSpec((samples, blk), lambda i: (0, i)),
            pl.BlockSpec((samples, batch), lambda i: (0, 0)),
            pl.BlockSpec((samples, batch), lambda i: (0, 0)),
        ],
        out_specs=[
            pl.BlockSpec((samples, blk), lambda i: (0, i)),
            pl.BlockSpec((samples, blk), lambda i: (0, i)),
        ],
        out_shape=[jax.ShapeDtypeStruct((samples, count), F32)] * 2,
        scratch_shapes=[
            pltpu.VMEM((2, batch, WIDE), BF16),
            pltpu.VMEM((2, 2 * samples, batch), BF16),
            pltpu.VMEM((blk // WIDE * 2 * samples, batch), BF16),
        ],
        compiler_params=params(),
        cost_estimate=pl.CostEstimate(
            flops=5 * 10**9, bytes_accessed=4 * samples * count * 4, transcendentals=0
        ),
        name="update",
    )(start, index, hbm(coeffs), hbm(velocity), grad0, grad1)


def exchange(blocks, axes):
    return lax.all_to_all(blocks, axes, 0, 0, tiled=True)


def copies(tile, size):
    return jnp.broadcast_to(tile[None], (size,) + tile.shape)


def after(values, *others):
    return lax.optimization_barrier((values, others))[0]


def per_device(n_rows, n_cols, points, coeffs, velocity, targets, batch_index, test_points):
    feats, count = points.shape
    samples = coeffs.shape[0]
    slab = test_points.shape[1]
    slab_tiles = slab // 128
    devices = n_rows * n_cols
    col = lax.axis_index("cols").astype(jnp.int32).reshape(1)
    start = (lax.axis_index(BOTH) * count).astype(jnp.int32).reshape(1)

    tests = test_points.reshape(feats, slab_tiles, 128).transpose(1, 0, 2).reshape(-1, 128)
    mine = gather_points(start, batch_index, points)
    part = exchange(mine, "rows")
    points, coeffs, velocity, targets = after((points, coeffs, velocity, targets), mine)
    sides, halves = prepare(points, coeffs, velocity)
    part, coeffs, velocity, targets = after((part, coeffs, velocity, targets), sides)
    part = jnp.sum(part, axis=0)
    part = exchange(copies(jnp.concatenate([part, tests], axis=0), n_cols), "cols")
    terms = gather_terms(start, batch_index, coeffs, velocity, targets)
    part, sides, halves = after((part, sides, halves), terms)
    tests = part[:, feats:].reshape(-1, feats, 128)
    part = jnp.sum(part[:, :feats], axis=0)
    drawn = exchange(copies(part, n_rows), "rows")
    sides, halves = after((sides, halves), part)
    test_part = test_sums(col, 0, n_cols, slab, 1, test_points, sides, halves, None)
    drawn, tests = after((drawn, tests), test_part)

    sums = batch_sums(drawn, sides, halves, terms)
    part = exchange(sums.reshape(devices, 8, 128), BOTH)
    test_part = after(test_part, sums)
    test_part = test_sums(col, 1, n_cols, slab, 2, tests, sides, halves, test_part)
    part, test_part = after((part, test_part))
    part = jnp.sum(part, axis=0)
    received = exchange(copies(part, devices), BOTH)
    test_part = test_sums(col, 3, n_cols, slab, 1, tests, sides, halves, test_part)
    received, test_part = after((received, test_part))
    received = received.reshape(-1, samples // 8, 8, 128)

    test_part = exchange(test_part.reshape(devices, 8, 128), BOTH)
    grads = second_gradient(drawn, batch_index, received)
    test_part, coeffs, velocity, grad0, grad1 = after((test_part, coeffs, velocity, *grads))
    test_part = jnp.sum(test_part, axis=0)
    test_part = exchange(copies(test_part, n_rows), "rows")
    coeffs_out, velocity_out = update(start, batch_index, coeffs, velocity, grad0, grad1)
    test_part, grad0, grad1 = after((test_part, grad0, grad1), coeffs_out)
    dense = test_part.reshape(samples // 8, slab_tiles, 8, 128)
    return (coeffs_out, velocity_out, test_change(test_points, drawn, grad0, grad1, dense))


def solution(mesh):
    n_rows, n_cols = mesh.shape["rows"], mesh.shape["cols"]
    return jax.shard_map(
        functools.partial(per_device, n_rows, n_cols),
        mesh=mesh,
        in_specs=(
            P(None, BOTH),
            P(None, BOTH),
            P(None, BOTH),
            P(None, BOTH),
            P(),
            P(None, "cols"),
        ),
        out_specs=(P(None, BOTH), P(None, BOTH), P(None, "cols")),
        check_vma=False,
    )
```

```python
import functools
import math

import jax
import jax.numpy as jnp
from jax import lax
from jax.experimental import pallas as pl
from jax.experimental.pallas import tpu as pltpu
from jax.sharding import PartitionSpec as P

BOTH = ("rows", "cols")
SCALE = 3.0**0.5 / 1.25
UNIT = SCALE / math.log(2.0)
SHIFT = 1.0 / math.log(2.0)
DROP = math.log2(math.log(2.0))
DEPTH = 144
WIDE = 256
F32 = jnp.float32
BF16 = jnp.bfloat16


def split(x, parts):
    pieces = []
    for _ in range(parts - 1):
        piece = x.astype(BF16)
        pieces.append(piece)
        x = x - piece.astype(F32)
    pieces.append(x.astype(BF16))
    return pieces


def side(points, scale):
    x = points * UNIT
    half = x.shape[0] // 2
    squares = x * x
    squares = split(squares[:half] + squares[half:], 3)
    return split(scale * x, 3), [piece.astype(F32) for piece in squares]


def rows_of(*parts):
    return jnp.concatenate(parts, axis=0).astype(BF16)


def point_side(points):
    (a, b, c), (d, e, f) = side(points, 1.0)
    one = jnp.ones(d.shape, F32)
    tail = [rows_of(d, e), rows_of(f, one), rows_of(one, one)]
    return jnp.concatenate([a, a, b, a, b, c] + tail, axis=0)


def query_side(queries):
    (a, b, c), (d, e, f) = side(queries, -2.0)
    one = jnp.ones(d.shape, F32)
    tail = [rows_of(one, one), rows_of(one, d), rows_of(e, f)]
    return jnp.concatenate([a, b, a, c, b, a] + tail, axis=0)


def transposed(x):
    return x.astype(F32).T.astype(BF16)


def matern(u_sq):
    u_sq = jnp.maximum(u_sq, 1e-12)
    u = u_sq * lax.rsqrt(u_sq)
    return (u + SHIFT) * jnp.exp2(DROP - u)


def last_dims(a, b):
    return lax.dot_general(a, b, (((1,), (1,)), ((), ())), preferred_element_type=F32)


def hbm(x):
    return pltpu.with_memory_space_constraint(x, pltpu.HBM)


def vmem(x):
    return pltpu.with_memory_space_constraint(x, pltpu.VMEM)


def params(mebibytes):
    return pltpu.CompilerParams(vmem_limit_bytes=mebibytes << 20)


def cost(evaluations):
    return pl.CostEstimate(
        flops=evaluations * 1024, bytes_accessed=1 << 20, transcendentals=2 * evaluations
    )


def lanes(tiles):
    return jnp.concatenate([tiles[i] for i in range(tiles.shape[0])], axis=1)


def store_columns(out, value):
    for i in range(out.shape[0]):
        out[i] = value[:, i * 128 : (i + 1) * 128]


def prepare_kernel(points, coeffs, velocity, sides, early, late):
    blk = 1024
    for first in range(0, points.shape[1], blk):
        cols = slice(first, first + blk)
        sides[:, cols] = point_side(points[:, cols])
        c = coeffs[:, cols]
        early[0, :, cols] = c.astype(BF16)
        v = 0.9 * velocity[:, cols]
        c = c + v
        early[1, :, cols] = c.astype(BF16)
        late[:, cols] = (c + 0.9 * v).astype(BF16)


def prepare(points, coeffs, velocity):
    count = points.shape[1]
    samples = coeffs.shape[0]
    whole = pl.BlockSpec(memory_space=pltpu.VMEM)
    return pl.pallas_call(
        prepare_kernel,
        in_specs=[whole, whole, whole],
        out_specs=[whole, whole, whole],
        out_shape=[
            pltpu.VMEM((DEPTH, count), BF16),
            jax.ShapeDtypeStruct((2, samples, count), BF16),
            jax.ShapeDtypeStruct((samples, count), BF16),
        ],
        compiler_params=params(8),
        name="prepare",
    )(points, coeffs, velocity)


def select_owned(stack, local, rows, parts):
    blocks = stack.shape[0] // rows
    q = local.shape[1]
    low = jnp.bitwise_and(local, WIDE - 1)
    high = jnp.right_shift(local, WIDE.bit_length() - 1)
    hot = (lax.broadcasted_iota(jnp.int32, (WIDE, q), 0) == low).astype(F32).astype(BF16)
    picked = jnp.dot(
        stack[...], jnp.concatenate([hot] * parts, axis=0), preferred_element_type=F32
    )
    total = jnp.zeros((rows, q), F32)
    for block in range(blocks):
        total = total + jnp.where(high == block, picked[block * rows : (block + 1) * rows], 0.0)
    return total


def fill_stack(stack, value_of, rows, parts):
    for block in range(stack.shape[0] // rows):
        pieces = split(value_of(slice(block * WIDE, (block + 1) * WIDE)), parts)
        for part, piece in enumerate(pieces):
            stack[block * rows : (block + 1) * rows, part * WIDE : (part + 1) * WIDE] = piece


def index_part(index, out):
    q = out.shape[0] * 128
    per_row = index.shape[1] // q
    step = pl.program_id(0)
    first = pl.multiple_of(lax.rem(step, per_row) * q, q)
    both = index[:, pl.ds(first, q)]
    return jnp.where(step < per_row, both[0:1], both[1:2])


def gather_points_kernel(start, index, points, out, stack):
    rows = points.shape[0]

    @pl.when(pl.program_id(0) == 0)
    def _():
        fill_stack(stack, lambda cols: points[:, cols], rows, 3)

    store_columns(out, select_owned(stack, index_part(index, out) - start[0], rows, 3))


def gather_points(start, index, points):
    feats, count = points.shape
    blk = 1024
    steps = index.size // blk
    return pl.pallas_call(
        gather_points_kernel,
        grid=(steps,),
        in_specs=[
            pl.BlockSpec(memory_space=pltpu.SMEM),
            pl.BlockSpec(index.shape, lambda i: (0, 0)),
            pl.BlockSpec((feats, count), lambda i: (0, 0)),
        ],
        out_specs=pl.BlockSpec((blk // 128, feats, 128), lambda i: (i, 0, 0)),
        out_shape=jax.ShapeDtypeStruct((steps * blk // 128, feats, 128), F32),
        scratch_shapes=[pltpu.VMEM((count // WIDE * feats, 3 * WIDE), BF16)],
        compiler_params=params(16),
        name="gather_points",
    )(start, hbm(index), hbm(points))


def gather_terms_kernel(half_steps, start, index, coeffs, velocity, targets, out, stack):
    rows = coeffs.shape[0]

    @pl.when(pl.program_id(0) == 0)
    def _():
        fill_stack(stack, lambda cols: coeffs[:, cols] - targets[:, cols], rows, 2)

    @pl.when(pl.program_id(0) == half_steps)
    def _():
        fill_stack(
            stack,
            lambda cols: coeffs[:, cols] + 0.9 * velocity[:, cols] - targets[:, cols],
            rows,
            2,
        )

    store_columns(out, select_owned(stack, index_part(index, out) - start[0], rows, 2))


def gather_terms(start, index, coeffs, velocity, targets):
    samples, count = coeffs.shape
    blk = 1024
    steps = index.size // blk
    whole = pl.BlockSpec((samples, count), lambda i: (0, 0))
    return pl.pallas_call(
        functools.partial(gather_terms_kernel, steps // 2),
        grid=(steps,),
        in_specs=[
            pl.BlockSpec(memory_space=pltpu.SMEM),
            pl.BlockSpec(index.shape, lambda i: (0, 0)),
            whole,
            whole,
            whole,
        ],
        out_specs=pl.BlockSpec((blk // 128, samples, 128), lambda i: (i, 0, 0)),
        out_shape=jax.ShapeDtypeStruct((steps * blk // 128, samples, 128), F32),
        scratch_shapes=[pltpu.VMEM((count // WIDE * samples, 2 * WIDE), BF16)],
        compiler_params=params(28),
        name="gather_terms",
    )(start, hbm(index), hbm(coeffs), hbm(velocity), hbm(targets))


def kernel_sums(side_t, sides, halves, chunk, unroll):
    count = sides.shape[1]
    q = side_t.shape[0]

    def step(i, acc):
        cols = pl.ds(pl.multiple_of(i * chunk, chunk), chunk)
        u_sq = jnp.dot(side_t[...], sides[:, cols], preferred_element_type=F32)
        return acc + last_dims(halves[:, cols], matern(u_sq).astype(BF16))

    return lax.fori_loop(
        0, count // chunk, step, jnp.zeros((halves.shape[0], q), F32), unroll=unroll
    )


def batch_kernel(queries, sides, halves, terms, out, side_t):
    side_t[...] = transposed(query_side(lanes(queries)))
    total = kernel_sums(side_t, sides, halves.at[0], 256, 16)
    for i in range(out.shape[0]):
        out[i] = total[:, i * 128 : (i + 1) * 128] + terms[i]


def batch_sums(drawn, sides, halves, terms):
    tiles, feats, _ = drawn.shape
    _, samples, count = halves.shape
    wide = 16
    steps = tiles // wide
    tile = pl.BlockSpec((wide, samples, 128), lambda i: (i, 0, 0))
    return pl.pallas_call(
        batch_kernel,
        grid=(steps,),
        in_specs=[
            pl.BlockSpec((wide, feats, 128), lambda i: (i, 0, 0)),
            pl.BlockSpec(memory_space=pltpu.VMEM),
            pl.BlockSpec((1, samples, count), lambda i: (i // (steps // 2), 0, 0)),
            tile,
        ],
        out_specs=tile,
        out_shape=jax.ShapeDtypeStruct(terms.shape, F32),
        scratch_shapes=[pltpu.VMEM((wide * 128, DEPTH), BF16)],
        compiler_params=params(32),
        cost_estimate=cost(tiles * 128 * count),
        name="batch_sums",
    )(drawn, vmem(sides), hbm(halves), terms)


def test_kernel(own, slab, queries, sides, halves, *refs):
    out, side_t = refs[-2:]
    side_t[...] = transposed(query_side(queries[...] if own else lanes(queries)))
    total = kernel_sums(side_t, sides, halves, 256, 16)
    for i in range(out.shape[0]):
        for j in range(out.shape[1]):
            out[i, j, 0] = total[i * 8 : (i + 1) * 8, j * 128 : (j + 1) * 128]


def test_sums(slab, offset, n_slabs, per_slab, many, queries, sides, halves, before):
    samples, count = halves.shape
    own = before is None
    slab_tiles = per_slab // 128

    def which(i, slab_ref):
        return lax.rem(slab_ref[0] + offset + i, n_slabs)

    if own:
        first = pl.BlockSpec((queries.shape[0], per_slab), lambda i, s: (0, 0))
    else:
        first = pl.BlockSpec(
            (slab_tiles, queries.shape[1], 128), lambda i, s: (which(i, s), 0, 0)
        )
    in_specs = [
        first,
        pl.BlockSpec(memory_space=pltpu.VMEM),
        pl.BlockSpec((samples, count), lambda i, s: (0, 0)),
    ]
    args = [queries, vmem(sides), hbm(halves)]
    aliases = {}
    if not own:
        in_specs.append(pl.BlockSpec(memory_space=pl.ANY))
        args.append(before)
        aliases = {4: 0}
    return pl.pallas_call(
        functools.partial(test_kernel, own),
        grid_spec=pltpu.PrefetchScalarGridSpec(
            num_scalar_prefetch=1,
            grid=(many,),
            in_specs=in_specs,
            out_specs=pl.BlockSpec(
                (samples // 8, slab_tiles, 1, 8, 128),
                lambda i, s: (0, 0, which(i, s), 0, 0),
            ),
            scratch_shapes=[pltpu.VMEM((per_slab, DEPTH), BF16)],
        ),
        out_shape=jax.ShapeDtypeStruct((samples // 8, slab_tiles, n_slabs, 8, 128), F32),
        input_output_aliases=aliases,
        compiler_params=params(20),
        cost_estimate=cost(many * per_slab * count),
        name="test_sums",
    )(slab, *args)


def tile_rows(tiles, i):
    return jnp.concatenate([tiles[i, j] for j in range(tiles.shape[1])], axis=0)


def second_kernel(drawn, index, received, grad0, grad1, sides, weights, side_t, col):
    batch = index.shape[1]
    tiles = batch // 128
    for tile in range(tiles):
        cols = slice(tile * 128, (tile + 1) * 128)
        sides[:, cols] = point_side(drawn[tile])
        side_t[cols, :] = transposed(query_side(drawn[tiles + tile]))
        g = tile_rows(received, tile)
        grad0[:, cols] = g
        weights[:, cols] = jnp.concatenate(split(-0.5 * g, 2), axis=0)
    col[...] = jnp.broadcast_to(index[1:2, :].astype(F32), (128, batch)).T
    chunk = 256
    total = jnp.zeros((weights.shape[0], batch), F32)
    for first in range(0, batch, chunk):
        cols = slice(first, first + chunk)
        u_sq = jnp.dot(side_t[...], sides[:, cols], preferred_element_type=F32)
        there = jnp.concatenate([col[...]] * (chunk // 128), axis=1)
        same = jnp.where(there == index[0:1, cols].astype(F32), 1.0, 0.0)
        kern = (matern(u_sq) + same).astype(BF16)
        total = total + last_dims(weights[:, cols], kern)
    half = weights.shape[0] // 2
    total = total[:half] + total[half:]
    for tile in range(tiles):
        cols = slice(tile * 128, (tile + 1) * 128)
        grad1[:, cols] = tile_rows(received, tiles + tile) + total[:, cols]


def second_gradient(drawn, index, received):
    batch = index.shape[1]
    samples = received.shape[1] * received.shape[2]
    return pl.pallas_call(
        second_kernel,
        out_shape=[jax.ShapeDtypeStruct((samples, batch), F32)] * 2,
        scratch_shapes=[
            pltpu.VMEM((DEPTH, batch), BF16),
            pltpu.VMEM((2 * samples, batch), BF16),
            pltpu.VMEM((batch, DEPTH), BF16),
            pltpu.VMEM((batch, 128), F32),
        ],
        compiler_params=params(26),
        cost_estimate=cost(batch * batch),
        name="second_gradient",
    )(drawn, index, received)


def test_tile_kernel(row, queries, drawn, grad0, grad1, out, sides, weights, side_t):
    batch = grad0.shape[1]
    across = queries.shape[1] // 128
    i, j = row[0] // across, lax.rem(row[0], across)
    for tile in range(drawn.shape[0]):
        sides[:, tile * 128 : (tile + 1) * 128] = point_side(drawn[tile])
    samples = pl.ds(pl.multiple_of(i * 8, 8), 8)
    for no, (grad, factor) in enumerate(((grad0, -0.95), (grad1, -0.5))):
        high, low = split(factor * grad[samples, :], 2)
        weights[:, no * batch : (no + 1) * batch] = rows_of(high.astype(F32), low.astype(F32))
    cols = pl.ds(pl.multiple_of(j * 128, 128), 128)
    side_t[...] = transposed(query_side(queries[:, cols]))
    change = kernel_sums(side_t, sides, weights, 1024, 2)
    out[...] = change[:8] + change[8:]


def test_tile(row, queries, drawn, grad0, grad1):
    whole = pl.BlockSpec(memory_space=pltpu.VMEM)
    total = drawn.shape[0] * 128
    return pl.pallas_call(
        test_tile_kernel,
        in_specs=[pl.BlockSpec(memory_space=pltpu.SMEM)] + [whole] * 4,
        out_shape=jax.ShapeDtypeStruct((8, 128), F32),
        scratch_shapes=[
            pltpu.VMEM((DEPTH, total), BF16),
            pltpu.VMEM((16, total), BF16),
            pltpu.VMEM((128, DEPTH), BF16),
        ],
        compiler_params=params(20),
        cost_estimate=cost(total * 128),
        name="test_tile",
    )(row, queries, drawn, grad0, grad1)


def add_tiles_kernel(change, parts, out):
    total = change[...]
    for part in range(parts.shape[0]):
        total = total + parts[part]
    for copy in range(out.shape[0]):
        out[copy] = total


def add_tiles(change, parts, copies_out):
    return pl.pallas_call(
        add_tiles_kernel,
        in_specs=[
            pl.BlockSpec(change.shape, lambda: (0, 0)),
            pl.BlockSpec(parts.shape, lambda: (0, 0, 0)),
        ],
        out_shape=jax.ShapeDtypeStruct((copies_out,) + change.shape, F32),
        compiler_params=params(8),
        name="add_tiles",
    )(change, hbm(parts))


def update_kernel(
    start, index, coeffs, velocity, grad0, grad1, coeffs_out, velocity_out, hot, pieces, masked
):
    samples, batch = grad0.shape
    block_cols = coeffs.shape[1] // WIDE
    local = index[...] - start[0]
    high = jnp.right_shift(local, WIDE.bit_length() - 1)

    @pl.when(pl.program_id(0) == 0)
    def _():
        low = jnp.bitwise_and(local, WIDE - 1).astype(F32)
        lane = lax.broadcasted_iota(jnp.int32, (batch, 128), 1).astype(F32)
        for step, grad in enumerate((grad0, grad1)):
            column = jnp.broadcast_to(low[step : step + 1], (128, batch)).T
            for part in range(WIDE // 128):
                hot[step, :, part * 128 : (part + 1) * 128] = (
                    (column == lane + part * 128.0).astype(F32).astype(BF16)
                )
            first, second = split(grad[...], 2)
            pieces[step, :samples] = first
            pieces[step, samples:] = second

    first_block = pl.program_id(0) * block_cols
    sums = []
    for step in range(2):
        for block in range(block_cols):
            here = (high[step : step + 1] == first_block + block).astype(F32)
            here = jnp.broadcast_to(here, (16, batch)).astype(BF16)
            for part in range(2 * samples // 16):
                row = block * 2 * samples + part * 16
                masked[row : row + 16] = pieces[step, part * 16 : (part + 1) * 16] * here
        sums.append(jnp.dot(masked[...], hot[step], preferred_element_type=F32))
    for block in range(block_cols):
        cols = slice(block * WIDE, (block + 1) * WIDE)
        top = block * 2 * samples
        g0, g1 = (s[top : top + samples] + s[top + samples : top + 2 * samples] for s in sums)
        v1 = 0.9 * velocity[:, cols] - 0.5 * g0
        c1 = coeffs[:, cols] + v1
        v2 = 0.9 * v1 - 0.5 * g1
        velocity_out[:, cols] = v2
        coeffs_out[:, cols] = c1 + v2


def update(start, index, coeffs, velocity, grad0, grad1):
    samples, count = coeffs.shape
    batch = grad0.shape[1]
    blk = min(count, 2048)
    return pl.pallas_call(
        update_kernel,
        grid=(count // blk,),
        in_specs=[
            pl.BlockSpec(memory_space=pltpu.SMEM),
            pl.BlockSpec((2, batch), lambda i: (0, 0)),
            pl.BlockSpec((samples, blk), lambda i: (0, i)),
            pl.BlockSpec((samples, blk), lambda i: (0, i)),
            pl.BlockSpec((samples, batch), lambda i: (0, 0)),
            pl.BlockSpec((samples, batch), lambda i: (0, 0)),
        ],
        out_specs=[
            pl.BlockSpec((samples, blk), lambda i: (0, i)),
            pl.BlockSpec((samples, blk), lambda i: (0, i)),
        ],
        out_shape=[jax.ShapeDtypeStruct((samples, count), F32)] * 2,
        scratch_shapes=[
            pltpu.VMEM((2, batch, WIDE), BF16),
            pltpu.VMEM((2, 2 * samples, batch), BF16),
            pltpu.VMEM((blk // WIDE * 2 * samples, batch), BF16),
        ],
        compiler_params=params(16),
        cost_estimate=pl.CostEstimate(
            flops=5 * 10**9, bytes_accessed=4 * samples * count * 4, transcendentals=0
        ),
        name="update",
    )(start, hbm(index), hbm(coeffs), hbm(velocity), grad0, grad1)


def exchange(blocks, axes):
    return lax.all_to_all(blocks, axes, 0, 0, tiled=True)


def copies(tile, size):
    return jnp.broadcast_to(tile[None], (size,) + tile.shape)


def after(values, *others):
    return lax.optimization_barrier((values, others))[0]


def per_device(n_rows, n_cols, points, coeffs, velocity, targets, batch_index, test_points):
    feats, count = points.shape
    samples = coeffs.shape[0]
    slab = test_points.shape[1]
    slab_tiles = slab // 128
    devices = n_rows * n_cols
    row = lax.axis_index("rows").astype(jnp.int32).reshape(1)
    col = lax.axis_index("cols").astype(jnp.int32).reshape(1)
    start = (lax.axis_index(BOTH) * count).astype(jnp.int32).reshape(1)

    tests = test_points.reshape(feats, slab_tiles, 128).transpose(1, 0, 2).reshape(-1, 128)
    mine = gather_points(start, batch_index, points)
    part = exchange(mine, "rows")
    points, coeffs, velocity, targets = after((points, coeffs, velocity, targets), mine)
    sides, early, late = prepare(points, coeffs, velocity)
    part, coeffs, velocity, targets = after((part, coeffs, velocity, targets), sides)
    part = jnp.sum(part, axis=0)
    part = exchange(copies(jnp.concatenate([part, tests], axis=0), n_cols), "cols")
    terms = gather_terms(start, batch_index, coeffs, velocity, targets)
    part, sides = after((part, sides), terms)
    tests = part[:, feats:].reshape(-1, feats, 128)
    part = jnp.sum(part[:, :feats], axis=0)
    drawn = exchange(copies(part, n_rows), "rows")
    sides = after(sides, part)
    test_part = test_sums(col, 0, n_cols, slab, 1, test_points, sides, late, None)
    drawn, tests = after((drawn, tests), test_part)

    sums = batch_sums(drawn, sides, early, terms)
    part = exchange(sums.reshape(devices, 8, 128), BOTH)
    test_part = after(test_part, sums)
    test_part = test_sums(col, 1, n_cols, slab, 2, tests, sides, late, test_part)
    part, test_part = after((part, test_part))
    part = jnp.sum(part, axis=0)
    received = exchange(copies(part, devices), BOTH)
    test_part = test_sums(col, 3, n_cols, slab, 1, tests, sides, late, test_part)
    received, test_part = after((received, test_part))
    received = received.reshape(-1, samples // 8, 8, 128)

    test_part = exchange(test_part.reshape(devices, 8, 128), BOTH)
    grads = second_gradient(drawn, batch_index, received)
    grad0, grad1 = grads
    change = test_tile(row, test_points, drawn, grad0, grad1)
    test_part = after(test_part, change)
    tile = add_tiles(change, test_part, n_rows)
    tiles = exchange(tile, "rows")
    coeffs, velocity, grad0, grad1 = after((coeffs, velocity, grad0, grad1), tile)
    coeffs_out, velocity_out = update(start, batch_index, coeffs, velocity, grad0, grad1)
    tiles = after(tiles, coeffs_out).reshape(samples // 8, slab_tiles, 8, 128)
    return (coeffs_out, velocity_out, tiles.transpose(0, 2, 1, 3).reshape(samples, slab))


def solution(mesh):
    n_rows, n_cols = mesh.shape["rows"], mesh.shape["cols"]
    return jax.shard_map(
        functools.partial(per_device, n_rows, n_cols),
        mesh=mesh,
        in_specs=(
            P(None, BOTH),
            P(None, BOTH),
            P(None, BOTH),
            P(None, BOTH),
            P(),
            P(None, "cols"),
        ),
        out_specs=(P(None, BOTH), P(None, BOTH), P(None, "cols")),
        check_vma=False,
    )
```

```python
import functools
import math

import jax
import jax.numpy as jnp
from jax import lax
from jax.experimental import pallas as pl
from jax.experimental.pallas import tpu as pltpu
from jax.sharding import PartitionSpec as P

BOTH = ("rows", "cols")
SCALE = 3.0**0.5 / 1.25
UNIT = SCALE / math.log(2.0)
SHIFT = 1.0 / math.log(2.0)
DROP = math.log2(math.log(2.0))
DEPTH = 144
WIDE = 256
F32 = jnp.float32
BF16 = jnp.bfloat16


def split(x, parts):
    pieces = []
    for _ in range(parts - 1):
        piece = x.astype(BF16)
        pieces.append(piece)
        x = x - piece.astype(F32)
    pieces.append(x.astype(BF16))
    return pieces


def side(points, scale):
    x = points * UNIT
    half = x.shape[0] // 2
    squares = x * x
    squares = split(squares[:half] + squares[half:], 3)
    return split(scale * x, 3), [piece.astype(F32) for piece in squares]


def rows_of(*parts):
    return jnp.concatenate(parts, axis=0).astype(BF16)


def point_side(points):
    (a, b, c), (d, e, f) = side(points, 1.0)
    one = jnp.ones(d.shape, F32)
    tail = [rows_of(d, e), rows_of(f, one), rows_of(one, one)]
    return jnp.concatenate([a, a, b, a, b, c] + tail, axis=0)


def query_side(queries):
    (a, b, c), (d, e, f) = side(queries, -2.0)
    one = jnp.ones(d.shape, F32)
    tail = [rows_of(one, one), rows_of(one, d), rows_of(e, f)]
    return jnp.concatenate([a, b, a, c, b, a] + tail, axis=0)


def transposed(x):
    return x.astype(F32).T.astype(BF16)


def matern(u_sq):
    u_sq = jnp.maximum(u_sq, 1e-12)
    u = u_sq * lax.rsqrt(u_sq)
    return (u + SHIFT) * jnp.exp2(DROP - u)


def last_dims(a, b):
    return lax.dot_general(a, b, (((1,), (1,)), ((), ())), preferred_element_type=F32)


def hbm(x):
    return pltpu.with_memory_space_constraint(x, pltpu.HBM)


def vmem(x):
    return pltpu.with_memory_space_constraint(x, pltpu.VMEM)


def params(mebibytes):
    return pltpu.CompilerParams(vmem_limit_bytes=mebibytes << 20)


def cost(evaluations):
    return pl.CostEstimate(
        flops=evaluations * 1024, bytes_accessed=1 << 20, transcendentals=2 * evaluations
    )


def lanes(tiles):
    return jnp.concatenate([tiles[i] for i in range(tiles.shape[0])], axis=1)


def store_columns(out, value):
    for i in range(out.shape[0]):
        out[i] = value[:, i * 128 : (i + 1) * 128]


def prepare_kernel(points, coeffs, velocity, sides, early, late):
    blk = 1024
    for first in range(0, points.shape[1], blk):
        cols = slice(first, first + blk)
        sides[:, cols] = point_side(points[:, cols])
        c = coeffs[:, cols]
        early[0, :, cols] = c.astype(BF16)
        v = 0.9 * velocity[:, cols]
        c = c + v
        early[1, :, cols] = c.astype(BF16)
        late[:, cols] = (c + 0.9 * v).astype(BF16)


def prepare(points, coeffs, velocity):
    count = points.shape[1]
    samples = coeffs.shape[0]
    whole = pl.BlockSpec(memory_space=pltpu.VMEM)
    return pl.pallas_call(
        prepare_kernel,
        in_specs=[whole, whole, whole],
        out_specs=[whole, whole, whole],
        out_shape=[
            pltpu.VMEM((DEPTH, count), BF16),
            jax.ShapeDtypeStruct((2, samples, count), BF16),
            jax.ShapeDtypeStruct((samples, count), BF16),
        ],
        compiler_params=params(8),
        name="prepare",
    )(points, coeffs, velocity)


def select_owned(stack, local, rows, parts):
    blocks = stack.shape[0] // rows
    q = local.shape[1]
    low = jnp.bitwise_and(local, WIDE - 1)
    high = jnp.right_shift(local, WIDE.bit_length() - 1)
    hot = (lax.broadcasted_iota(jnp.int32, (WIDE, q), 0) == low).astype(F32).astype(BF16)
    picked = jnp.dot(
        stack[...], jnp.concatenate([hot] * parts, axis=0), preferred_element_type=F32
    )
    total = jnp.zeros((rows, q), F32)
    for block in range(blocks):
        total = total + jnp.where(high == block, picked[block * rows : (block + 1) * rows], 0.0)
    return total


def fill_stack(stack, value_of, rows, parts):
    for block in range(stack.shape[0] // rows):
        pieces = split(value_of(slice(block * WIDE, (block + 1) * WIDE)), parts)
        for part, piece in enumerate(pieces):
            stack[block * rows : (block + 1) * rows, part * WIDE : (part + 1) * WIDE] = piece


def index_part(index, out):
    q = out.shape[0] * 128
    per_row = index.shape[1] // q
    step = pl.program_id(0)
    first = pl.multiple_of(lax.rem(step, per_row) * q, q)
    both = index[:, pl.ds(first, q)]
    return jnp.where(step < per_row, both[0:1], both[1:2])


def gather_points_kernel(start, index, points, out, stack):
    rows = points.shape[0]

    @pl.when(pl.program_id(0) == 0)
    def _():
        fill_stack(stack, lambda cols: points[:, cols], rows, 3)

    store_columns(out, select_owned(stack, index_part(index, out) - start[0], rows, 3))


def gather_points(start, index, points):
    feats, count = points.shape
    blk = 2048
    steps = index.size // blk
    return pl.pallas_call(
        gather_points_kernel,
        grid=(steps,),
        in_specs=[
            pl.BlockSpec(memory_space=pltpu.SMEM),
            pl.BlockSpec(index.shape, lambda i: (0, 0)),
            pl.BlockSpec((feats, count), lambda i: (0, 0)),
        ],
        out_specs=pl.BlockSpec((blk // 128, feats, 128), lambda i: (i, 0, 0)),
        out_shape=jax.ShapeDtypeStruct((steps * blk // 128, feats, 128), F32),
        scratch_shapes=[pltpu.VMEM((count // WIDE * feats, 3 * WIDE), BF16)],
        compiler_params=params(28),
        name="gather_points",
    )(start, hbm(index), hbm(points))


def gather_terms_kernel(half_steps, start, index, coeffs, velocity, targets, out, stack):
    rows = coeffs.shape[0]

    @pl.when(pl.program_id(0) == 0)
    def _():
        fill_stack(stack, lambda cols: coeffs[:, cols] - targets[:, cols], rows, 2)

    @pl.when(pl.program_id(0) == half_steps)
    def _():
        fill_stack(
            stack,
            lambda cols: coeffs[:, cols] + 0.9 * velocity[:, cols] - targets[:, cols],
            rows,
            2,
        )

    store_columns(out, select_owned(stack, index_part(index, out) - start[0], rows, 2))


def gather_terms(start, index, coeffs, velocity, targets):
    samples, count = coeffs.shape
    blk = 1024
    steps = index.size // blk
    whole = pl.BlockSpec((samples, count), lambda i: (0, 0))
    return pl.pallas_call(
        functools.partial(gather_terms_kernel, steps // 2),
        grid=(steps,),
        in_specs=[
            pl.BlockSpec(memory_space=pltpu.SMEM),
            pl.BlockSpec(index.shape, lambda i: (0, 0)),
            whole,
            whole,
            whole,
        ],
        out_specs=pl.BlockSpec((blk // 128, samples, 128), lambda i: (i, 0, 0)),
        out_shape=jax.ShapeDtypeStruct((steps * blk // 128, samples, 128), F32),
        scratch_shapes=[pltpu.VMEM((count // WIDE * samples, 2 * WIDE), BF16)],
        compiler_params=params(28),
        name="gather_terms",
    )(start, hbm(index), hbm(coeffs), hbm(velocity), hbm(targets))


def kernel_sums(side_t, sides, halves, chunk, unroll):
    count = sides.shape[1]
    q = side_t.shape[0]

    def step(i, acc):
        cols = pl.ds(pl.multiple_of(i * chunk, chunk), chunk)
        u_sq = jnp.dot(side_t[...], sides[:, cols], preferred_element_type=F32)
        return acc + last_dims(halves[:, cols], matern(u_sq).astype(BF16))

    return lax.fori_loop(
        0, count // chunk, step, jnp.zeros((halves.shape[0], q), F32), unroll=unroll
    )


def batch_kernel(queries, sides, halves, terms, out, side_t):
    side_t[...] = transposed(query_side(lanes(queries)))
    total = kernel_sums(side_t, sides, halves.at[0], 256, 16)
    for i in range(out.shape[0]):
        out[i] = total[:, i * 128 : (i + 1) * 128] + terms[i]


def batch_sums(drawn, sides, halves, terms):
    tiles, feats, _ = drawn.shape
    _, samples, count = halves.shape
    wide = 16
    steps = tiles // wide
    tile = pl.BlockSpec((wide, samples, 128), lambda i: (i, 0, 0))
    return pl.pallas_call(
        batch_kernel,
        grid=(steps,),
        in_specs=[
            pl.BlockSpec((wide, feats, 128), lambda i: (i, 0, 0)),
            pl.BlockSpec(memory_space=pltpu.VMEM),
            pl.BlockSpec((1, samples, count), lambda i: (i // (steps // 2), 0, 0)),
            tile,
        ],
        out_specs=tile,
        out_shape=jax.ShapeDtypeStruct(terms.shape, F32),
        scratch_shapes=[pltpu.VMEM((wide * 128, DEPTH), BF16)],
        compiler_params=params(32),
        cost_estimate=cost(tiles * 128 * count),
        name="batch_sums",
    )(drawn, vmem(sides), hbm(halves), terms)


def test_kernel(own, slab, queries, sides, halves, *refs):
    out, side_t = refs[-2:]
    side_t[...] = transposed(query_side(queries[...] if own else lanes(queries)))
    total = kernel_sums(side_t, sides, halves, 256, 16)
    for i in range(out.shape[0]):
        for j in range(out.shape[1]):
            out[i, j, 0] = total[i * 8 : (i + 1) * 8, j * 128 : (j + 1) * 128]


def test_sums(slab, offset, n_slabs, per_slab, many, queries, sides, halves, before):
    samples, count = halves.shape
    own = before is None
    slab_tiles = per_slab // 128

    def which(i, slab_ref):
        return lax.rem(slab_ref[0] + offset + i, n_slabs)

    if own:
        first = pl.BlockSpec((queries.shape[0], per_slab), lambda i, s: (0, 0))
    else:
        first = pl.BlockSpec(
            (slab_tiles, queries.shape[1], 128), lambda i, s: (which(i, s), 0, 0)
        )
    in_specs = [
        first,
        pl.BlockSpec(memory_space=pltpu.VMEM),
        pl.BlockSpec((samples, count), lambda i, s: (0, 0)),
    ]
    args = [queries, vmem(sides), hbm(halves)]
    aliases = {}
    if not own:
        in_specs.append(pl.BlockSpec(memory_space=pl.ANY))
        args.append(before)
        aliases = {4: 0}
    return pl.pallas_call(
        functools.partial(test_kernel, own),
        grid_spec=pltpu.PrefetchScalarGridSpec(
            num_scalar_prefetch=1,
            grid=(many,),
            in_specs=in_specs,
            out_specs=pl.BlockSpec(
                (samples // 8, slab_tiles, 1, 8, 128),
                lambda i, s: (0, 0, which(i, s), 0, 0),
            ),
            scratch_shapes=[pltpu.VMEM((per_slab, DEPTH), BF16)],
        ),
        out_shape=jax.ShapeDtypeStruct((samples // 8, slab_tiles, n_slabs, 8, 128), F32),
        input_output_aliases=aliases,
        compiler_params=params(20),
        cost_estimate=cost(many * per_slab * count),
        name="test_sums",
    )(slab, *args)


def tile_rows(tiles, i):
    return jnp.concatenate([tiles[i, j] for j in range(tiles.shape[1])], axis=0)


def second_kernel(drawn, index, received, grad0, grad1, sides, weights, side_t, col):
    batch = index.shape[1]
    tiles = batch // 128
    for tile in range(tiles):
        cols = slice(tile * 128, (tile + 1) * 128)
        sides[:, cols] = point_side(drawn[tile])
        side_t[cols, :] = transposed(query_side(drawn[tiles + tile]))
        g = tile_rows(received, tile)
        grad0[:, cols] = g
        weights[:, cols] = jnp.concatenate(split(-0.5 * g, 2), axis=0)
    col[...] = jnp.broadcast_to(index[1:2, :].astype(F32), (128, batch)).T
    chunk = 256
    total = jnp.zeros((weights.shape[0], batch), F32)
    for first in range(0, batch, chunk):
        cols = slice(first, first + chunk)
        u_sq = jnp.dot(side_t[...], sides[:, cols], preferred_element_type=F32)
        there = jnp.concatenate([col[...]] * (chunk // 128), axis=1)
        same = jnp.where(there == index[0:1, cols].astype(F32), 1.0, 0.0)
        kern = (matern(u_sq) + same).astype(BF16)
        total = total + last_dims(weights[:, cols], kern)
    half = weights.shape[0] // 2
    total = total[:half] + total[half:]
    for tile in range(tiles):
        cols = slice(tile * 128, (tile + 1) * 128)
        grad1[:, cols] = tile_rows(received, tiles + tile) + total[:, cols]


def second_gradient(drawn, index, received):
    batch = index.shape[1]
    samples = received.shape[1] * received.shape[2]
    return pl.pallas_call(
        second_kernel,
        out_shape=[jax.ShapeDtypeStruct((samples, batch), F32)] * 2,
        scratch_shapes=[
            pltpu.VMEM((DEPTH, batch), BF16),
            pltpu.VMEM((2 * samples, batch), BF16),
            pltpu.VMEM((batch, DEPTH), BF16),
            pltpu.VMEM((batch, 128), F32),
        ],
        compiler_params=params(26),
        cost_estimate=cost(batch * batch),
        name="second_gradient",
    )(drawn, index, received)


def test_tile_kernel(row, queries, drawn, grad0, grad1, out, sides, weights, side_t):
    batch = grad0.shape[1]
    across = queries.shape[1] // 128
    i, j = row[0] // across, lax.rem(row[0], across)
    for tile in range(drawn.shape[0]):
        sides[:, tile * 128 : (tile + 1) * 128] = point_side(drawn[tile])
    samples = pl.ds(pl.multiple_of(i * 8, 8), 8)
    for no, (grad, factor) in enumerate(((grad0, -0.95), (grad1, -0.5))):
        high, low = split(factor * grad[samples, :], 2)
        weights[:, no * batch : (no + 1) * batch] = rows_of(high.astype(F32), low.astype(F32))
    cols = pl.ds(pl.multiple_of(j * 128, 128), 128)
    side_t[...] = transposed(query_side(queries[:, cols]))
    change = kernel_sums(side_t, sides, weights, 1024, 2)
    out[...] = change[:8] + change[8:]


def test_tile(row, queries, drawn, grad0, grad1):
    whole = pl.BlockSpec(memory_space=pltpu.VMEM)
    total = drawn.shape[0] * 128
    return pl.pallas_call(
        test_tile_kernel,
        in_specs=[pl.BlockSpec(memory_space=pltpu.SMEM)] + [whole] * 4,
        out_shape=jax.ShapeDtypeStruct((8, 128), F32),
        scratch_shapes=[
            pltpu.VMEM((DEPTH, total), BF16),
            pltpu.VMEM((16, total), BF16),
            pltpu.VMEM((128, DEPTH), BF16),
        ],
        compiler_params=params(20),
        cost_estimate=cost(total * 128),
        name="test_tile",
    )(row, queries, drawn, grad0, grad1)


def sum_copies_kernel(parts, out):
    total = parts[0]
    for part in range(1, parts.shape[0]):
        total = total + parts[part]
    for copy in range(out.shape[0]):
        out[copy] = total


def sum_copies(parts, copies_out):
    return pl.pallas_call(
        sum_copies_kernel,
        in_specs=[pl.BlockSpec(memory_space=pltpu.VMEM)],
        out_shape=jax.ShapeDtypeStruct((copies_out,) + parts.shape[1:], F32),
        compiler_params=params(8),
        name="sum_copies",
    )(parts)


def update_kernel(
    start, index, coeffs, velocity, grad0, grad1, coeffs_out, velocity_out, hot, pieces, masked
):
    samples, batch = grad0.shape
    block_cols = coeffs.shape[1] // WIDE
    local = index[...] - start[0]
    high = jnp.right_shift(local, WIDE.bit_length() - 1)

    @pl.when(pl.program_id(0) == 0)
    def _():
        low = jnp.bitwise_and(local, WIDE - 1).astype(F32)
        lane = lax.broadcasted_iota(jnp.int32, (batch, 128), 1).astype(F32)
        for step, grad in enumerate((grad0, grad1)):
            column = jnp.broadcast_to(low[step : step + 1], (128, batch)).T
            for part in range(WIDE // 128):
                hot[step, :, part * 128 : (part + 1) * 128] = (
                    (column == lane + part * 128.0).astype(F32).astype(BF16)
                )
            first, second = split(grad[...], 2)
            pieces[step, :samples] = first
            pieces[step, samples:] = second

    first_block = pl.program_id(0) * block_cols
    sums = []
    for step in range(2):
        for block in range(block_cols):
            here = (high[step : step + 1] == first_block + block).astype(F32)
            here = jnp.broadcast_to(here, (16, batch)).astype(BF16)
            for part in range(2 * samples // 16):
                row = block * 2 * samples + part * 16
                masked[row : row + 16] = pieces[step, part * 16 : (part + 1) * 16] * here
        sums.append(jnp.dot(masked[...], hot[step], preferred_element_type=F32))
    for block in range(block_cols):
        cols = slice(block * WIDE, (block + 1) * WIDE)
        top = block * 2 * samples
        g0, g1 = (s[top : top + samples] + s[top + samples : top + 2 * samples] for s in sums)
        v1 = 0.9 * velocity[:, cols] - 0.5 * g0
        c1 = coeffs[:, cols] + v1
        v2 = 0.9 * v1 - 0.5 * g1
        velocity_out[:, cols] = v2
        coeffs_out[:, cols] = c1 + v2


def update(start, index, coeffs, velocity, grad0, grad1):
    samples, count = coeffs.shape
    batch = grad0.shape[1]
    blk = min(count, 2048)
    return pl.pallas_call(
        update_kernel,
        grid=(count // blk,),
        in_specs=[
            pl.BlockSpec(memory_space=pltpu.SMEM),
            pl.BlockSpec((2, batch), lambda i: (0, 0)),
            pl.BlockSpec((samples, blk), lambda i: (0, i)),
            pl.BlockSpec((samples, blk), lambda i: (0, i)),
            pl.BlockSpec((samples, batch), lambda i: (0, 0)),
            pl.BlockSpec((samples, batch), lambda i: (0, 0)),
        ],
        out_specs=[
            pl.BlockSpec((samples, blk), lambda i: (0, i)),
            pl.BlockSpec((samples, blk), lambda i: (0, i)),
        ],
        out_shape=[jax.ShapeDtypeStruct((samples, count), F32)] * 2,
        scratch_shapes=[
            pltpu.VMEM((2, batch, WIDE), BF16),
            pltpu.VMEM((2, 2 * samples, batch), BF16),
            pltpu.VMEM((blk // WIDE * 2 * samples, batch), BF16),
        ],
        compiler_params=params(16),
        cost_estimate=pl.CostEstimate(
            flops=5 * 10**9, bytes_accessed=4 * samples * count * 4, transcendentals=0
        ),
        name="update",
    )(start, hbm(index), hbm(coeffs), hbm(velocity), grad0, grad1)


def exchange(blocks, axes):
    return lax.all_to_all(blocks, axes, 0, 0, tiled=True)


def copies(tile, size):
    return jnp.broadcast_to(tile[None], (size,) + tile.shape)


def after(values, *others):
    return lax.optimization_barrier((values, others))[0]


def per_device(n_rows, n_cols, points, coeffs, velocity, targets, batch_index, test_points):
    feats, count = points.shape
    samples = coeffs.shape[0]
    slab = test_points.shape[1]
    slab_tiles = slab // 128
    devices = n_rows * n_cols
    row = lax.axis_index("rows").astype(jnp.int32).reshape(1)
    col = lax.axis_index("cols").astype(jnp.int32).reshape(1)
    start = (lax.axis_index(BOTH) * count).astype(jnp.int32).reshape(1)

    tests = test_points.reshape(feats, slab_tiles, 128).transpose(1, 0, 2).reshape(-1, 128)
    mine = gather_points(start, batch_index, points)
    part = exchange(mine, "rows")
    points, coeffs, velocity, targets = after((points, coeffs, velocity, targets), mine)
    sides, early, late = prepare(points, coeffs, velocity)
    part, coeffs, velocity, targets = after((part, coeffs, velocity, targets), sides)
    part = jnp.sum(part, axis=0)
    part = exchange(copies(jnp.concatenate([part, tests], axis=0), n_cols), "cols")
    terms = gather_terms(start, batch_index, coeffs, velocity, targets)
    part, sides = after((part, sides), terms)
    tests = part[:, feats:].reshape(-1, feats, 128)
    part = jnp.sum(part[:, :feats], axis=0)
    drawn = exchange(copies(part, n_rows), "rows")
    sides = after(sides, part)
    test_part = test_sums(col, 0, n_cols, slab, 1, test_points, sides, late, None)
    drawn, tests = after((drawn, tests), test_part)

    sums = batch_sums(drawn, sides, early, terms)
    part = exchange(sums.reshape(devices, 8, 128), BOTH)
    test_part = after(test_part, sums)
    test_part = test_sums(col, 1, n_cols, slab, 2, tests, sides, late, test_part)
    part, test_part = after((part, test_part))
    received = exchange(sum_copies(part, devices), BOTH)
    test_part = test_sums(col, 3, n_cols, slab, 1, tests, sides, late, test_part)
    received, test_part = after((received, test_part))
    received = received.reshape(-1, samples // 8, 8, 128)

    test_part = exchange(test_part.reshape(devices, 8, 128), BOTH)
    grads = second_gradient(drawn, batch_index, received)
    grad0, grad1 = grads
    change = test_tile(row, test_points, drawn, grad0, grad1)
    test_part = after(test_part, change)
    tile = copies(jnp.sum(test_part, axis=0) + change, n_rows)
    tiles = exchange(tile, "rows")
    coeffs, velocity, grad0, grad1 = after((coeffs, velocity, grad0, grad1), tile)
    coeffs_out, velocity_out = update(start, batch_index, coeffs, velocity, grad0, grad1)
    tiles = after(tiles, coeffs_out).reshape(samples // 8, slab_tiles, 8, 128)
    return (coeffs_out, velocity_out, tiles.transpose(0, 2, 1, 3).reshape(samples, slab))


def solution(mesh):
    n_rows, n_cols = mesh.shape["rows"], mesh.shape["cols"]
    return jax.shard_map(
        functools.partial(per_device, n_rows, n_cols),
        mesh=mesh,
        in_specs=(
            P(None, BOTH),
            P(None, BOTH),
            P(None, BOTH),
            P(None, BOTH),
            P(),
            P(None, "cols"),
        ),
        out_specs=(P(None, BOTH), P(None, BOTH), P(None, "cols")),
        check_vma=False,
    )
```
